768 devices in a mesh: sec: 192 (over z_lo, x, y, core), col: 4 (over z_hi).
Axes of the slice: x: 4, y: 8, z: 12 (z_hi: 4, z_lo: 3; z = z_hi * 3 + z_lo), core: 2. Of those that a mesh axis runs over, the one named last changes fastest.
Arguments:
- air_state: float32 [4, 64, 786432], P(None, None, ('sec', 'col')), may hold values from -6 to 6
- air_mix: float32 [64, 786432], P(None, ('sec', 'col')), may hold values from 0.1 to 4
- surface_forcing: float32 [4, 786432], P(None, ('sec', 'col')), may hold values from 0 to 2
- air_mask: int32 [786432], P(('sec', 'col')), may hold values 0 or 1
- ocean_sources: int32 [4, 786432], P(None, ('sec', 'col')), may hold values from 0 to 6143, as said below
- ocean_weights: float32 [4, 786432], P(None, ('sec', 'col')), may hold values from 0.1 to 0.5
- sea_state: float32 [2, 80, 393216], P(None, None, ('sec', 'col')), may hold values from -6 to 6
- sea_mix: float32 [80, 393216], P(None, ('sec', 'col')), may hold values from 0.1 to 4
- ice_cover: float32 [393216], P(('sec', 'col')), may hold values from 0.05 to 0.95
- sea_mask: int32 [393216], P(('sec', 'col')), may hold values 0 or 1
- air_sources: int32 [4, 393216], P(None, ('sec', 'col')), may hold values from 0 to 12287, as said below
- air_weights: float32 [4, 393216], P(None, ('sec', 'col')), may hold values from 0.1 to 0.5
Outputs:
- air_out: float32 [4, 64, 786432], P(None, None, ('sec', 'col'))
- sea_out: float32 [2, 80, 393216], P(None, None, ('sec', 'col'))
- ice_out: float32 [393216], P(('sec', 'col'))
The draws below stay inside these ranges and needn't reach their ends.
Inputs may be any that keep to these rules, and one draw needn't show every extreme that they name: Section t holds ocean cells t * 2048 to (t + 1) * 2048 - 1 and atmosphere columns t * 4096 to (t + 1) * 4096 - 1. An entry s of ocean_sources names cell s mod 2048 of the section s // 2048 - 1 places after the column's own. An entry s of air_sources names column s mod 4096 of the section s // 4096 - 1 places after the cell's own.
All inputs are finite; a program needn't handle non-finite values. No bound on the sum of `air_mask` or of `sea_mask` on one device may be relied on, other than what follows from the above.
Results may differ from the reference program's by a relative error of at most 0.0001.
Values sent between devices are 32-bit elements; how exact they have to be, the bound alone decides.
A program may use at most 64 MiB of HBM per device.

```python
import math
import jax
import jax.numpy as jnp
from jax import lax

LEV = 64
OLEV = 80
KA = 4
KO = 4
STEPS = 2
SECA = 4096
SECO = 2048
ACOLS = 786432
OCELLS = 393216


def draw_ocean_sources(key, part):
    key_band, key_cell = jax.random.split(jax.random.fold_in(key, 17))
    offset = jax.random.randint(key_band, (KO, ACOLS), 0, 3)
    within = jax.random.randint(key_cell, (KO, ACOLS), 0, SECO)
    return (offset * SECO + within).astype(jnp.int32)


def draw_air_sources(key, part):
    key_band, key_cell = jax.random.split(jax.random.fold_in(key, 29))
    offset = jax.random.randint(key_band, (KA, OCELLS), 0, 3)
    within = jax.random.randint(key_cell, (KA, OCELLS), 0, SECA)
    return (offset * SECA + within).astype(jnp.int32)


def set_ends(drawn, key, smallest, top_value):
    longest = drawn.shape.index(max(drawn.shape))
    spots = []
    for shift in (0, 1):
        where = [jax.random.randint(jax.random.fold_in(key, axis), (), 0, length) for axis, length in enumerate(drawn.shape)]
        where[longest] = (where[longest] + shift) % drawn.shape[longest]
        spots.append(tuple(where))
    return drawn.at[spots[0]].set(smallest).at[spots[1]].set(top_value)


def block_scale(key, shape, shards, least, largest):
    gain, own = 1.0, jax.random.fold_in(key, 6)
    for dim, shards_of in shards:
        draws = jnp.exp(jax.random.uniform(jax.random.fold_in(own, dim), (shards_of,), jnp.float32, least / len(shards), largest / len(shards)))
        gain = gain * jnp.repeat(draws, shape[dim] // shards_of).reshape([-1 if axis == dim else 1 for axis in range(len(shape))])
    return gain


def bell_draw(stream_key, extent, deviation, reach, cuts=(), kind=jnp.bfloat16):
    drawn = deviation * jax.random.normal(stream_key, extent, jnp.float32)
    if cuts:
        drawn = drawn * block_scale(stream_key, extent, cuts, -0.22, 0.18)
    return jnp.clip(drawn, -reach, reach).astype(kind)


def setup_inputs(seed: int = 0) -> dict:
    keys = jax.random.split(jax.random.key(seed), 13)
    air_state = bell_draw(keys[0], (4, LEV, ACOLS), 1.0, 6.0, ((2, 768),), jnp.float32)
    air_mix = jnp.clip(jnp.exp(math.log(4.0) - 3.6888794 * jax.random.uniform(keys[1], (LEV, ACOLS), jnp.float32) ** block_scale(keys[1], (LEV, ACOLS), ((1, 768),), -0.2, 0.2)), 0.1, 4.0)
    surface_forcing = jnp.clip(2.0 * jax.random.uniform(keys[2], (4, ACOLS), jnp.float32) ** block_scale(keys[2], (4, ACOLS), ((1, 768),), -0.2, 0.2), 0.0, 2.0)
    air_mask = set_ends((jax.random.randint(keys[3], (ACOLS,), 0, 3) < 2).astype(jnp.int32), jax.random.fold_in(keys[3], 1), 0, 1)
    ocean_sources = draw_ocean_sources(jax.random.fold_in(keys[12], 71), 0)
    ocean_weights = jnp.clip(0.1 + 0.4 * jax.random.uniform(keys[5], (KO, ACOLS), jnp.float32) ** block_scale(keys[5], (KO, ACOLS), ((1, 768),), -0.2, 0.2), 0.1, 0.5)
    sea_state = bell_draw(keys[6], (2, OLEV, OCELLS), 1.0, 6.0, ((2, 768),), jnp.float32)
    sea_mix = jnp.clip(jnp.exp(math.log(4.0) - 3.6888794 * jax.random.uniform(keys[7], (OLEV, OCELLS), jnp.float32) ** block_scale(keys[7], (OLEV, OCELLS), ((1, 768),), -0.2, 0.2)), 0.1, 4.0)
    ice_cover = jnp.clip(0.05 + 0.9 * jax.random.uniform(keys[8], (OCELLS,), jnp.float32) ** block_scale(keys[8], (OCELLS,), ((0, 768),), -0.2, 0.2), 0.05, 0.95)
    sea_mask = set_ends((jax.random.randint(keys[9], (OCELLS,), 0, 4) < 3).astype(jnp.int32), jax.random.fold_in(keys[9], 1), 0, 1)
    air_sources = draw_air_sources(jax.random.fold_in(keys[12], 71), 0)
    air_weights = jnp.clip(0.1 + 0.4 * jax.random.uniform(keys[11], (KA, OCELLS), jnp.float32) ** block_scale(keys[11], (KA, OCELLS), ((1, 768),), -0.2, 0.2), 0.1, 0.5)
    return dict(air_state=air_state, air_mix=air_mix, surface_forcing=surface_forcing, air_mask=air_mask, ocean_sources=ocean_sources, ocean_weights=ocean_weights, sea_state=sea_state, sea_mix=sea_mix, ice_cover=ice_cover, sea_mask=sea_mask, air_sources=air_sources, air_weights=air_weights)


def solve_columns(mixing, right_side):
    column_depth = mixing.shape[0]
    zeros_row = jnp.zeros_like(mixing[0])
    carry_c = zeros_row
    carry_d = jnp.zeros_like(right_side[:, 0])
    ratios = []
    reduced = []
    for depth_index in range(column_depth):
        lower_k = mixing[depth_index - 1] if depth_index > 0 else zeros_row
        upper_k = mixing[depth_index]
        pivot_value = 1.0 + lower_k + upper_k + lower_k * carry_c
        carry_c = -upper_k / pivot_value
        carry_d = (right_side[:, depth_index] + lower_k * carry_d) / pivot_value
        ratios.append(carry_c)
        reduced.append(carry_d)
    current = reduced[-1]
    solved = [current]
    for depth_index in range(column_depth - 2, -1, -1):
        current = reduced[depth_index] - ratios[depth_index] * current
        solved.append(current)
    return jnp.stack(solved[::-1], axis=1)

def global_places(sources, home_span, source_span, section_count):
    owners = jnp.arange(sources.shape[1], dtype=jnp.int32) // home_span
    band = jnp.mod(owners[None, :] - 1 + sources // source_span, section_count)
    return (band * source_span + sources % source_span).astype(jnp.int32)

def remap(values, sources, weights):
    return lax.optimization_barrier(jnp.sum(weights[None] * values[:, sources], axis=1))

def surface_fluxes(air_state, air_sea, surface_forcing, air_mask):
    bottom = air_state[:, 0]
    over_sea = air_mask == 1
    skin = jnp.where(over_sea, air_sea[0], surface_forcing[3])
    frozen = jnp.where(over_sea, air_sea[1], 0.0)
    speed = jnp.sqrt(bottom[2] * bottom[2] + bottom[3] * bottom[3] + 1.0)
    coefficient = 0.3 * speed / (1.0 + frozen)
    snow_part = 1.0 / (1.0 + jnp.exp(2.0 * skin))
    return jnp.stack([coefficient * (skin - bottom[0]), coefficient * (0.5 * jnp.exp(0.3 * skin) - bottom[1]), coefficient * bottom[2], coefficient * bottom[3], surface_forcing[0] / (1.0 + frozen), surface_forcing[1] - 0.2 * skin, surface_forcing[2] * (1.0 - snow_part), surface_forcing[2] * snow_part])

def air_step(air_state, air_mix, fluxes):
    bottom_add = jnp.stack([fluxes[0], fluxes[1], -fluxes[2], -fluxes[3]])
    return solve_columns(air_mix, air_state.at[:, 0].add(bottom_add))

def sea_step(sea_state, sea_mix, ice_cover, sea_mask, sea_flux):
    stress = jnp.sqrt(sea_flux[2] * sea_flux[2] + sea_flux[3] * sea_flux[3] + 0.01)
    heat = sea_flux[4] + sea_flux[5] - sea_flux[0] - sea_flux[1]
    open_water = 1.0 - ice_cover
    depth_decay = jnp.exp(-jnp.arange(sea_mix.shape[0], dtype=jnp.float32) / 8.0)
    mixing = sea_mix * (1.0 + 2.0 * stress[None, :] * depth_decay[:, None])
    top_add = jnp.stack([0.5 * open_water * heat, 0.3 * open_water * (0.4 * sea_flux[1] - sea_flux[6])])
    solved = solve_columns(mixing, sea_state.at[:, 0].add(top_add))
    wet_cells = sea_mask == 1
    new_state = jnp.where(wet_cells[None, None], solved, sea_state)
    grown = ice_cover / (ice_cover + open_water * jnp.exp(0.5 * heat - 0.8 * sea_flux[7]))
    return (new_state, jnp.where(wet_cells, grown, ice_cover))

def reference(air_state, air_mix, surface_forcing, air_mask, ocean_sources, ocean_weights, sea_state, sea_mix, ice_cover, sea_mask, air_sources, air_weights):
    section_count = ACOLS // SECA
    ocean_cell = global_places(ocean_sources, SECA, SECO, section_count)
    air_column = global_places(air_sources, SECO, SECA, section_count)
    for step_index in range(STEPS):
        sea_top = jnp.stack([sea_state[0, 0], ice_cover])
        air_sea = remap(sea_top, ocean_cell, ocean_weights)
        fluxes = surface_fluxes(air_state, air_sea, surface_forcing, air_mask)
        air_state = air_step(air_state, air_mix, fluxes)
        sea_flux = remap(fluxes, air_column, air_weights)
        sea_state, ice_cover = sea_step(sea_state, sea_mix, ice_cover, sea_mask, sea_flux)
    return (air_state, sea_state, ice_cover)
```

```python
import functools

import jax
import jax.numpy as jnp
from jax import lax
from jax.experimental import pallas as pl
from jax.experimental.pallas import tpu as pltpu
from jax.sharding import PartitionSpec as P

STEPS = 2
COLS = 4
LEV = 64
OLEV = 80
MESH = pl.DeviceIdType.MESH
F32 = jnp.float32
GATHER = lax.GatherDimensionNumbers(
    offset_dims=(),
    collapsed_slice_dims=(1,),
    start_index_map=(1,),
    operand_batching_dims=(0,),
    start_indices_batching_dims=(0,),
)


def lanes(row, index):
    return lax.gather(
        jnp.broadcast_to(row, (8, 128)),
        index[:, :, None],
        GATHER,
        slice_sizes=(1, 1),
        mode=lax.GatherScatterMode.PROMISE_IN_BOUNDS,
    )


def twice(half):
    return jnp.concatenate([half, half], axis=0)


def kernel(
    sections,
    air_h, amix_h, forcing_h, amask_h, osrc_h, owt_h, sea_h, smix_h, ice_h, smask_h, asrc_h, awt_h,
    air_o, sea_o, ice_o,
    air_v, amix_v, forcing_v, amask_v, osrc_v, owt_v, sea_v, smix_v, ice_v, smask_v, asrc_v, awt_v,
    top_out, top_in, flux_in, part_acc, part_out, part_in,
    smix8, sdecay8, sea8, sq, sw, sa, sb,
    aq, aa, ag, ab, ae, ay, aw, air_w, sea_w, ice_w,
    load_sem, src_send, src_recv, wt_send, wt_recv,
    top_send, top_recv, flux_send, flux_recv, part_send, part_recv, out_sem,
):
    sec = lax.axis_index("sec")
    col = lax.axis_index("col")

    def peer(shift, turn):
        return (lax.rem(sec + shift + sections, sections), lax.rem(col + turn, COLS))

    others = [(s, t) for t in (2, 1, 3, 0) for s in (0, -1, 1) if (s, t) != (0, 0)]

    barrier = pltpu.get_barrier_semaphore()
    for place in others:
        pl.semaphore_signal(barrier, inc=1, device_id=peer(*place), device_id_type=MESH)

    loads = [
        pltpu.make_async_copy(src, dst, load_sem.at[i])
        for i, (src, dst) in enumerate(
            [
                (sea_h, sea_v), (ice_h, ice_v), (osrc_h, osrc_v), (owt_h, owt_v),
                (forcing_h, forcing_v), (amask_h, amask_v), (amix_h, amix_v), (air_h, air_v),
                (smix_h, smix_v), (smask_h, smask_v),
                (asrc_h, asrc_v.at[col]), (awt_h, awt_v.at[col]),
            ]
        )
    ]
    for load in loads:
        load.start()

    first = lax.broadcasted_iota(jnp.int32, (8, 128), 0) < 4
    waiting = []

    def send_top(step):
        for n, (shift, turn) in enumerate(others):
            copy = pltpu.make_async_remote_copy(
                src_ref=top_out.at[step],
                dst_ref=top_in.at[step, (1 - shift) * COLS + col],
                send_sem=top_send.at[step, n],
                recv_sem=top_recv.at[step, (1 - shift) * COLS + col],
                device_id=peer(shift, turn),
                device_id_type=MESH,
            )
            copy.start()
            waiting.append(copy)

    loads[0].wait()
    loads[1].wait()
    top_out[0] = jnp.concatenate([sea_v[pl.ds(0, 4, stride=8), :], ice_v[...]], axis=0)
    pl.semaphore_wait(barrier, len(others))
    send_top(0)
    for turn in (2, 1, 3):
        for src, dst, send, recv in ((asrc_h, asrc_v, src_send, src_recv), (awt_h, awt_v, wt_send, wt_recv)):
            copy = pltpu.make_async_remote_copy(
                src_ref=src,
                dst_ref=dst.at[col],
                send_sem=send.at[turn],
                recv_sem=recv.at[col],
                device_id=peer(0, turn),
                device_id_type=MESH,
            )
            copy.start()
            waiting.append(copy)

    for load in loads[2:10]:
        load.wait()

    def air_up(n, carry):
        tile = 7 - n
        p, q = carry
        for s in range(7, -1, -1):
            k = amix_v[pl.ds(tile * 64 + s, 8, stride=8), :]
            b = 1.0 / (1.0 + k)
            a = k * b
            aq_next = q
            flow = a * q
            q = b * p + flow
            p = p + flow
            level = pl.ds(pl.multiple_of(tile * 64 + s * 8, 8), 8)
            below = pl.ds(pl.multiple_of(tile * 64 + s * 8 + 8, 8), 8)
            aq[level, :] = q
            aa[level, :] = a
            r = 1.0 / q
            ag[below, :] = a * aq_next * r
            ab[below, :] = b * r
        return p, q

    one = jnp.ones((8, 128), F32)
    zero = jnp.zeros((8, 128), F32)
    pa, qa = lax.fori_loop(0, LEV // 8, air_up, (one, zero))
    inv_pa = 1.0 / pa

    def air_solve(load):
        def up(n, w):
            tile = 7 - n
            w = list(w)
            for s in range(7, -1, -1):
                row = pl.multiple_of(tile * 64 + s * 8, 8)
                q, a = aq[pl.ds(row, 8), :], aa[pl.ds(row, 8), :]
                e = load(tile, s)
                for f in range(4):
                    w[f] = q * e[f] + a * w[f]
                    aw[f, pl.ds(row, 8), :] = w[f]
            return tuple(w)

        return [v * inv_pa for v in lax.fori_loop(0, LEV // 8, up, (zero,) * 4)]

    def from_start(tile, s):
        return [air_v[pl.ds(f * 512 + tile * 64 + s, 8, stride=8), :] for f in range(4)]

    top = air_solve(from_start)
    unit = qa * inv_pa

    def air_down(tile, carry):
        x, e = list(carry[:4]), carry[4]
        for s in range(8):
            row = pl.multiple_of(tile * 64 + s * 8, 8)
            g, b = ag[pl.ds(row, 8), :], ab[pl.ds(row, 8), :]
            for f in range(4):
                x[f] = g * x[f] + b * aw[f, pl.ds(row, 8), :]
                ay[f, pl.ds(row, 8), :] = x[f]
            e = g * e
            ae[pl.ds(row, 8), :] = e
        return (*x, e)

    ag[pl.ds(0, 8), :] = one
    ab[pl.ds(0, 8), :] = zero
    lax.fori_loop(0, LEV // 8, air_down, (*top, unit))

    def sea_prepare(tile, carry):
        decay = jnp.exp(jnp.full((8, 128), -tile.astype(F32)))
        for s in range(8):
            row = pl.ds(pl.multiple_of(tile * 64 + s * 8, 8), 8)
            k = twice(smix_v[pl.ds(tile * 32 + s, 4, stride=8), :])
            smix8[row, :] = k
            sdecay8[row, :] = k * (decay * jnp.exp(jnp.full((8, 128), -s / 8.0, F32)))
            sea8[row, :] = jnp.concatenate(
                [sea_v[pl.ds(tile * 32 + s, 4, stride=8), :], sea_v[pl.ds(320 + tile * 32 + s, 4, stride=8), :]], axis=0
            )
        return carry

    lax.fori_loop(0, OLEV // 8, sea_prepare, 0)
    wet = twice(smask_v[...]) == 1
    ice = twice(ice_v[...])
    over_sea = amask_v[...] == 1
    forcing = [forcing_v[pl.ds(f, 8, stride=4), :] for f in range(4)]
    bottom = [air_v[pl.ds(f * 512, 8, stride=8), :] for f in range(4)]

    push = None
    for step in range(STEPS):
        last = step == STEPS - 1
        top_in[step, COLS + col] = top_out[step]
        source = [osrc_v[pl.ds(k, 8, stride=4), :] for k in range(4)]
        lane = [v & 127 for v in source]
        line = [v >> 7 for v in source]
        temps, ices = [zero] * 4, [zero] * 4
        for shift, turn in [(0, 0), *[(s, t) for t in (0, 1, 3, 2) for s in (0, -1, 1) if (s, t) != (0, 0)]]:
            slot = (1 + shift) * COLS + lax.rem(col + turn, COLS)
            if (shift, turn) != (0, 0):
                pltpu.make_async_copy(top_in.at[step, slot], top_in.at[step, slot], top_recv.at[step, slot]).wait()
            for c in range(4):
                t, i = top_in[step, slot, pl.ds(c, 1), :], top_in[step, slot, pl.ds(4 + c, 1), :]
                for k in range(4):
                    here = line[k] == slot * 4 + c
                    temps[k] = jnp.where(here, lanes(t, lane[k]), temps[k])
                    ices[k] = jnp.where(here, lanes(i, lane[k]), ices[k])
        weight = [owt_v[pl.ds(k, 8, stride=4), :] for k in range(4)]
        warm = (weight[0] * temps[0] + weight[1] * temps[1]) + (weight[2] * temps[2] + weight[3] * temps[3])
        cold = (weight[0] * ices[0] + weight[1] * ices[1]) + (weight[2] * ices[2] + weight[3] * ices[3])

        skin = jnp.where(over_sea, warm, forcing[3])
        frozen = jnp.where(over_sea, cold, 0.0)
        closed = 1.0 / (1.0 + frozen)
        speed = jnp.sqrt(bottom[2] * bottom[2] + bottom[3] * bottom[3] + 1.0)
        coef = 0.3 * speed * closed
        snow = 1.0 / (1.0 + jnp.exp(2.0 * skin))
        f0 = coef * (skin - bottom[0])
        f1 = coef * (0.5 * jnp.exp(0.3 * skin) - bottom[1])
        f2 = coef * bottom[2]
        f3 = coef * bottom[3]
        heat = forcing[0] * closed + (forcing[1] - 0.2 * skin) - f0 - f1
        salt = 0.4 * f1 - forcing[2] * (1.0 - snow)
        melt = 0.5 * heat - 0.8 * (forcing[2] * snow)
        for f, v in enumerate((f2, f3, heat, salt, melt)):
            flux_in[step, 1, f] = v
        for n, shift in enumerate((-1, 1)):
            copy = pltpu.make_async_remote_copy(
                src_ref=flux_in.at[step, 1],
                dst_ref=flux_in.at[step, 1 - shift],
                send_sem=flux_send.at[step, n],
                recv_sem=flux_recv.at[step, 1 - shift],
                device_id=peer(shift, 0),
                device_id_type=MESH,
            )
            copy.start()
            waiting.append(copy)
        push = (f0, f1, -f2, -f3)

        if step == 0:
            loads[10].wait()
            loads[11].wait()
            for turn in (1, 2, 3):
                slot = lax.rem(col + turn, COLS)
                pltpu.make_async_copy(asrc_v.at[slot], asrc_v.at[slot], src_recv.at[slot]).wait()
                pltpu.make_async_copy(awt_v.at[slot], awt_v.at[slot], wt_recv.at[slot]).wait()

        def picked(target, bands, sums):
            index = [asrc_v[target, pl.ds(8 * h, 8), :] for h in range(2)]
            lane = [v & 127 for v in index]
            line = [(v >> 7) - 8 * col for v in index]
            for band in bands:
                for j in range(8):
                    here = [line[h] == band * 32 + j for h in range(2)]
                    for f in range(5):
                        row = flux_in[step, band, f, pl.ds(j, 1), :]
                        for h in range(2):
                            sums[f * 2 + h] = jnp.where(here[h], lanes(row, lane[h]), sums[f * 2 + h])
            return sums

        def own_part(turn, carry):
            target = lax.rem(col + turn, COLS)
            for n, v in enumerate(picked(target, (1,), [zero] * 10)):
                part_acc[turn, n] = v
            return carry

        lax.fori_loop(0, COLS, own_part, 0)
        if last:
            def air_result(tile, carry):
                for s in range(8):
                    row = pl.multiple_of(tile * 64 + s * 8, 8)
                    e = ae[pl.ds(row, 8), :]
                    for f in range(4):
                        air_w[pl.ds(f * 512 + tile * 64 + s, 8, stride=8), :] = ay[f, pl.ds(row, 8), :] + e * push[f]
                return carry

            lax.fori_loop(0, LEV // 8, air_result, 0)
            air_copy = pltpu.make_async_copy(air_w, air_o, out_sem.at[0])
            air_copy.start()

        for band in (0, 2):
            pltpu.make_async_copy(flux_in.at[step, band], flux_in.at[step, band], flux_recv.at[step, band]).wait()

        def whole_part(target, turn):
            sums = picked(target, (0, 2), [part_acc[turn, n] for n in range(10)])
            for f in range(5):
                done = []
                for h in range(2):
                    v = sums[f * 2 + h] * awt_v[target, pl.ds(8 * h, 8), :]
                    v = v + pltpu.roll(v, 6, 0)
                    v = v + pltpu.roll(v, 7, 0)
                    done.append(v)
                part_out[step, turn, pl.ds(4 * f, 4), :] = jnp.concatenate(
                    [done[0][0:1], done[0][4:5], done[1][0:1], done[1][4:5]], axis=0
                )

        for turn in (2, 1, 3, 0):
            target = lax.rem(col + turn, COLS)
            whole_part(target, turn)
            if turn:
                copy = pltpu.make_async_remote_copy(
                    src_ref=part_out.at[step, turn],
                    dst_ref=part_in.at[step, COLS - turn],
                    send_sem=part_send.at[step, turn],
                    recv_sem=part_recv.at[step, COLS - turn],
                    device_id=peer(0, turn),
                    device_id_type=MESH,
                )
                copy.start()
                waiting.append(copy)

        if not last:
            bottom = [ay[f, pl.ds(0, 8), :] + ae[pl.ds(0, 8), :] * push[f] for f in range(4)]
            first_push = push

            def after_first(tile, s):
                row = pl.multiple_of(tile * 64 + s * 8, 8)
                return [ay[f, pl.ds(row, 8), :] + ae[pl.ds(row, 8), :] * first_push[f] for f in range(4)]

            top = air_solve(after_first)

        total = part_out[step, 0]
        for turn in (1, 3, 2):
            pltpu.make_async_copy(part_in.at[step, turn], part_in.at[step, turn], part_recv.at[step, turn]).wait()
            total = total + part_in[step, turn]
        f2, f3, heat, salt, melt = [total[4 * f : 4 * f + 4] for f in range(5)]

        stress = twice(2.0 * jnp.sqrt(f2 * f2 + f3 * f3 + 0.01))
        open_water = 1.0 - ice
        added = open_water * jnp.concatenate([0.5 * heat, 0.3 * salt], axis=0)
        sea8[pl.ds(0, 8), :] = sea8[pl.ds(0, 8), :] + jnp.where(wet, added, 0.0)

        def sea_up(n, carry):
            tile = OLEV // 8 - 1 - n
            p, q, w = carry
            for s in range(7, -1, -1):
                row = pl.ds(pl.multiple_of(tile * 64 + s * 8, 8), 8)
                k = smix8[row, :] + stress * sdecay8[row, :]
                b = 1.0 / (1.0 + k)
                a = k * b
                flow = a * q
                q = b * p + flow
                p = p + flow
                w = q * sea8[row, :] + a * w
                sa[row, :] = a
                sb[row, :] = b
                sq[row, :] = q
                sw[row, :] = w
            return p, q, w

        p, q, w = lax.fori_loop(0, OLEV // 8, sea_up, (one, zero, zero))
        surface = jnp.where(wet, w / p, sea8[pl.ds(0, 8), :])
        grown = ice / (ice + open_water * jnp.exp(twice(melt)))
        ice = jnp.where(wet, grown, ice)
        if not last:
            top_out[step + 1] = jnp.where(first, surface, ice)
            send_top(step + 1)
            lax.fori_loop(0, LEV // 8, functools.partial(air_down_again, ag, ab, aw, ay), tuple(top))
        else:
            ice_w[...] = ice[0:4]
            ice_copy = pltpu.make_async_copy(ice_w, ice_o, out_sem.at[2])
            ice_copy.start()

        def sea_level(row, x, q, a, b):
            here = sq[row, :]
            r = 1.0 / q
            x = (a * here * r) * x + (b * r) * sw[row, :]
            return x, here, sa[row, :], sb[row, :]

        def sea_keep(row, tile, s, x):
            x = jnp.where(wet, x, sea8[row, :])
            if last:
                sea_w[pl.ds(tile * 32 + s, 4, stride=8), :] = x[0:4]
                sea_w[pl.ds(320 + tile * 32 + s, 4, stride=8), :] = x[4:8]
            else:
                sea8[row, :] = x

        def sea_down(tile, carry):
            x, q, a, b = carry
            for s in range(8):
                row = pl.ds(pl.multiple_of(tile * 64 + s * 8, 8), 8)
                x, q, a, b = sea_level(row, x, q, a, b)
                sea_keep(row, tile, s, x)
            return x, q, a, b

        row = pl.ds(0, 8)
        sea_keep(row, 0, 0, surface)
        state = (w / p, sq[row, :], sa[row, :], sb[row, :])
        for s in range(1, 8):
            row = pl.ds(s * 8, 8)
            state = sea_level(row, *state)
            sea_keep(row, 0, s, state[0])
        lax.fori_loop(1, OLEV // 8, sea_down, state)

    sea_copy = pltpu.make_async_copy(sea_w, sea_o, out_sem.at[1])
    sea_copy.start()
    for copy in waiting:
        copy.wait_send()
    air_copy.wait()
    ice_copy.wait()
    sea_copy.wait()


def air_down_again(ag, ab, aw, ay, tile, carry):
    x = list(carry)
    for s in range(8):
        row = pl.ds(pl.multiple_of(tile * 64 + s * 8, 8), 8)
        g, b = ag[row, :], ab[row, :]
        for f in range(4):
            x[f] = g * x[f] + b * aw[f, row, :]
            ay[f, row, :] = x[f]
    return tuple(x)


def lines(value):
    levels, columns = value.shape[-2:]
    tall = min(8, levels)
    return value.reshape(-1, tall, columns // 128, 128).swapaxes(1, 2).reshape(-1, 128)


def unlines(rows, shape):
    levels, columns = shape[-2:]
    return rows.reshape(-1, columns // 128, 8, 128).swapaxes(1, 2).reshape(shape)


def per_device(sections, *args):
    air_state, air_mix, forcing, air_mask, osrc, owt, sea_state, sea_mix, ice, sea_mask, asrc, awt = args
    operands = [
        lines(air_state), lines(air_mix), lines(forcing), air_mask.reshape(8, 128), lines(osrc), lines(owt),
        lines(sea_state), lines(sea_mix), ice.reshape(4, 128), sea_mask.reshape(4, 128), lines(asrc), lines(awt),
    ]
    vmem = [pltpu.VMEM(v.shape, v.dtype) for v in operands[:10]]
    vmem += [pltpu.VMEM((COLS, *v.shape), v.dtype) for v in operands[10:]]
    dma = pltpu.SemaphoreType.DMA
    tall = pltpu.VMEM((8 * OLEV, 128), F32)
    air_one = pltpu.VMEM((8 * LEV, 128), F32)
    air_plus = pltpu.VMEM((8 * LEV + 8, 128), F32)
    air_four = pltpu.VMEM((4, 8 * LEV, 128), F32)
    outs = pl.pallas_call(
        functools.partial(kernel, sections),
        out_shape=[
            jax.ShapeDtypeStruct((2048, 128), F32),
            jax.ShapeDtypeStruct((640, 128), F32),
            jax.ShapeDtypeStruct((4, 128), F32),
        ],
        in_specs=[pl.BlockSpec(memory_space=pltpu.HBM)] * 12,
        out_specs=[pl.BlockSpec(memory_space=pl.ANY)] * 3,
        scratch_shapes=[
            *vmem,
            pltpu.VMEM((STEPS, 8, 128), F32),
            pltpu.VMEM((STEPS, 3 * COLS, 8, 128), F32),
            pltpu.VMEM((STEPS, 3, 5, 8, 128), F32),
            pltpu.VMEM((COLS, 10, 8, 128), F32),
            pltpu.VMEM((STEPS, COLS, 20, 128), F32),
            pltpu.VMEM((STEPS, COLS, 20, 128), F32),
            tall, tall, tall, tall, tall, tall, tall,
            air_one, air_one, air_plus, air_plus, air_one, air_four, air_four,
            pltpu.VMEM((2048, 128), F32), pltpu.VMEM((640, 128), F32), pltpu.VMEM((4, 128), F32),
            dma((12,)), dma((COLS,)), dma((COLS,)), dma((COLS,)), dma((COLS,)),
            dma((STEPS, 11)), dma((STEPS, 12)), dma((STEPS, 2)), dma((STEPS, 3)),
            dma((STEPS, COLS)), dma((STEPS, COLS)), dma((3,)),
        ],
        compiler_params=pltpu.CompilerParams(collective_id=0, has_side_effects=True, vmem_limit_bytes=60 * 2**20),
        cost_estimate=pl.CostEstimate(flops=20_000_000, bytes_accessed=4_000_000, transcendentals=100_000),
        name="coupled",
    )(*operands)
    return unlines(outs[0], air_state.shape), unlines(outs[1], sea_state.shape), outs[2].reshape(512)


def solution(mesh):
    whole = ("sec", "col")
    deep, flat, line = P(None, None, whole), P(None, whole), P(whole)
    return jax.shard_map(
        functools.partial(per_device, mesh.shape["sec"]),
        mesh=mesh,
        in_specs=(deep, flat, flat, line, flat, flat, deep, flat, line, line, flat, flat),
        out_specs=(deep, deep, line),
        check_vma=False,
    )
```

```python
import functools

import jax
import jax.numpy as jnp
from jax import lax
from jax.experimental import pallas as pl
from jax.experimental.pallas import tpu as pltpu
from jax.sharding import PartitionSpec as P

STEPS = 2
COLS = 4
LEV = 64
OLEV = 80
MESH = pl.DeviceIdType.MESH
F32 = jnp.float32
GATHER = lax.GatherDimensionNumbers(
    offset_dims=(),
    collapsed_slice_dims=(1,),
    start_index_map=(1,),
    operand_batching_dims=(0,),
    start_indices_batching_dims=(0,),
)


def lanes(row, index):
    return lax.gather(
        jnp.broadcast_to(row, (8, 128)),
        index[:, :, None],
        GATHER,
        slice_sizes=(1, 1),
        mode=lax.GatherScatterMode.PROMISE_IN_BOUNDS,
    )


def twice(half):
    return jnp.concatenate([half, half], axis=0)


def kernel(
    sections,
    air_h, amix_h, forcing_h, amask_h, osrc_h, owt_h, sea_h, smix_h, ice_h, smask_h, asrc_h, awt_h,
    air_o, sea_o, ice_o,
    air_v, amix_v, forcing_v, amask_v, osrc_v, owt_v, sea_v, smix_v, ice_v, smask_v, asrc_v, awt_v,
    top_out, top_in, flux_v, part_out, part_in, source_in, weight_in,
    smix8, sdecay8, sea8, sq, sw, sa, sb,
    aq, aa, ag, ab, ae, ay, aw, air_w, sea_w, ice_w,
    load_sem, top_send, top_recv, part_send, part_recv, src_send, src_recv, wt_send, wt_recv, out_sem,
):
    sec = lax.axis_index("sec")
    col = lax.axis_index("col")

    def peer(shift, turn):
        return (lax.rem(sec + shift + sections, sections), lax.rem(col + turn, COLS))

    others = [(-1, 2), (1, 2), (-1, 1), (1, 1), (-1, 3), (1, 3), (0, 2), (-1, 0), (1, 0), (0, 1), (0, 3)]

    barrier = pltpu.get_barrier_semaphore()
    for place in others:
        pl.semaphore_signal(barrier, inc=1, device_id=peer(*place), device_id_type=MESH)

    loads = [
        pltpu.make_async_copy(src, dst, load_sem.at[i])
        for i, (src, dst) in enumerate(
            [
                (sea_h, sea_v), (ice_h, ice_v), (osrc_h, osrc_v), (owt_h, owt_v),
                (forcing_h, forcing_v), (amask_h, amask_v), (amix_h, amix_v), (air_h, air_v),
                (smix_h, smix_v), (smask_h, smask_v),
                (asrc_h, asrc_v), (awt_h, awt_v),
            ]
        )
    ]
    for load in loads:
        load.start()

    one = jnp.ones((8, 128), F32)
    zero = jnp.zeros((8, 128), F32)
    first = lax.broadcasted_iota(jnp.int32, (8, 128), 0) < 4
    waiting = []

    def send(block, places, send_sem, recv_sem, make=None):
        for n, (shift, turn) in enumerate(others):
            slot = (1 - shift) * COLS + col
            copy = pltpu.make_async_remote_copy(
                src_ref=make(n, shift, turn) if make else block,
                dst_ref=places.at[slot],
                send_sem=send_sem.at[n],
                recv_sem=recv_sem.at[slot],
                device_id=peer(shift, turn),
                device_id_type=MESH,
            )
            copy.start()
            waiting.append(copy)

    def landed(shift, turn, places, recv_sem):
        slot = (1 + shift) * COLS + lax.rem(col + turn, COLS)
        block = places.at[slot]
        pltpu.make_async_copy(block, block, recv_sem.at[slot]).wait()
        return slot

    def arrivals(step, places, recv_sem, read, count):
        def one_turn(turn, sums):
            for shift in (0, -1, 1):
                slot = (1 + shift) * COLS + lax.rem(col + turn, COLS)
                if shift or not isinstance(turn, int):
                    landed(shift, turn, places.at[step], recv_sem.at[step])
                sums = read(slot, sums)
            return sums

        sums = one_turn(0, (zero,) * count)
        return lax.fori_loop(1, COLS, lambda n, sums: one_turn(n + n // 2 - 2 * (n // 3), sums), sums)

    loads[0].wait()
    loads[1].wait()
    top_out[0] = jnp.concatenate([sea_v[pl.ds(0, 4, stride=8), :], ice_v[...]], axis=0)
    pl.semaphore_wait(barrier, len(others))
    send(top_out.at[0], top_in.at[0], top_send.at[0], top_recv.at[0])
    loads[10].wait()
    loads[11].wait()
    for rows, places in ((asrc_v, source_in), (awt_v, weight_in)):
        four = [rows[pl.ds(k, 4, stride=4), :] for k in range(4)]
        places[COLS + col] = jnp.concatenate(four, axis=0)
    send(source_in.at[COLS + col], source_in, src_send, src_recv)
    send(weight_in.at[COLS + col], weight_in, wt_send, wt_recv)
    for load in loads[2:10]:
        load.wait()

    def air_up(n, carry):
        tile = 7 - n
        p, q = carry
        for s in range(7, -1, -1):
            k = amix_v[pl.ds(tile * 64 + s, 8, stride=8), :]
            b = 1.0 / (1.0 + k)
            a = k * b
            aq_next = q
            flow = a * q
            q = b * p + flow
            p = p + flow
            level = pl.ds(pl.multiple_of(tile * 64 + s * 8, 8), 8)
            below = pl.ds(pl.multiple_of(tile * 64 + s * 8 + 8, 8), 8)
            aq[level, :] = q
            aa[level, :] = a
            r = 1.0 / q
            ag[below, :] = a * aq_next * r
            ab[below, :] = b * r
        return p, q

    pa, qa = lax.fori_loop(0, LEV // 8, air_up, (one, zero))
    inv_pa = 1.0 / pa

    def air_solve(load):
        def up(n, w):
            tile = 7 - n
            w = list(w)
            for s in range(7, -1, -1):
                row = pl.multiple_of(tile * 64 + s * 8, 8)
                q, a = aq[pl.ds(row, 8), :], aa[pl.ds(row, 8), :]
                e = load(tile, s)
                for f in range(4):
                    w[f] = q * e[f] + a * w[f]
                    aw[f, pl.ds(row, 8), :] = w[f]
            return tuple(w)

        return [v * inv_pa for v in lax.fori_loop(0, LEV // 8, up, (zero,) * 4)]

    def from_start(tile, s):
        return [air_v[pl.ds(f * 512 + tile * 64 + s, 8, stride=8), :] for f in range(4)]

    top = air_solve(from_start)
    unit = qa * inv_pa

    def air_down(tile, carry):
        x, e = list(carry[:4]), carry[4]
        for s in range(8):
            row = pl.multiple_of(tile * 64 + s * 8, 8)
            g, b = ag[pl.ds(row, 8), :], ab[pl.ds(row, 8), :]
            for f in range(4):
                x[f] = g * x[f] + b * aw[f, pl.ds(row, 8), :]
                ay[f, pl.ds(row, 8), :] = x[f]
            e = g * e
            ae[pl.ds(row, 8), :] = e
        return (*x, e)

    ag[pl.ds(0, 8), :] = one
    ab[pl.ds(0, 8), :] = zero
    lax.fori_loop(0, LEV // 8, air_down, (*top, unit))

    def sea_prepare(tile, carry):
        decay = jnp.exp(jnp.full((8, 128), -tile.astype(F32)))
        for s in range(8):
            row = pl.ds(pl.multiple_of(tile * 64 + s * 8, 8), 8)
            k = twice(smix_v[pl.ds(tile * 32 + s, 4, stride=8), :])
            smix8[row, :] = k
            sdecay8[row, :] = k * (decay * jnp.exp(jnp.full((8, 128), -s / 8.0, F32)))
            sea8[row, :] = jnp.concatenate(
                [sea_v[pl.ds(tile * 32 + s, 4, stride=8), :], sea_v[pl.ds(320 + tile * 32 + s, 4, stride=8), :]], axis=0
            )
        return carry

    lax.fori_loop(0, OLEV // 8, sea_prepare, 0)
    wet = twice(smask_v[...]) == 1
    ice = twice(ice_v[...])

    over_sea = amask_v[...] == 1
    forcing = [forcing_v[pl.ds(f, 8, stride=4), :] for f in range(4)]
    bottom = [air_v[pl.ds(f * 512, 8, stride=8), :] for f in range(4)]

    push = None
    for step in range(STEPS):
        last = step == STEPS - 1
        top_in[step, COLS + col] = top_out[step]
        source = [osrc_v[pl.ds(k, 8, stride=4), :] for k in range(4)]
        lane = [v & 127 for v in source]
        line = [v >> 7 for v in source]
        def read_top(slot, sums):
            sums = list(sums)
            for c in range(4):
                t, i = top_in[step, slot, pl.ds(c, 1), :], top_in[step, slot, pl.ds(4 + c, 1), :]
                for k in range(4):
                    here = line[k] == slot * 4 + c
                    sums[k] = jnp.where(here, lanes(t, lane[k]), sums[k])
                    sums[4 + k] = jnp.where(here, lanes(i, lane[k]), sums[4 + k])
            return tuple(sums)

        picked = arrivals(step, top_in, top_recv, read_top, 8)
        temps, ices = picked[:4], picked[4:]
        weight = [owt_v[pl.ds(k, 8, stride=4), :] for k in range(4)]
        warm = (weight[0] * temps[0] + weight[1] * temps[1]) + (weight[2] * temps[2] + weight[3] * temps[3])
        cold = (weight[0] * ices[0] + weight[1] * ices[1]) + (weight[2] * ices[2] + weight[3] * ices[3])

        skin = jnp.where(over_sea, warm, forcing[3])
        frozen = jnp.where(over_sea, cold, 0.0)
        closed = 1.0 / (1.0 + frozen)
        speed = jnp.sqrt(bottom[2] * bottom[2] + bottom[3] * bottom[3] + 1.0)
        coef = 0.3 * speed * closed
        snow = 1.0 / (1.0 + jnp.exp(2.0 * skin))
        f0 = coef * (skin - bottom[0])
        f1 = coef * (0.5 * jnp.exp(0.3 * skin) - bottom[1])
        f2 = coef * bottom[2]
        f3 = coef * bottom[3]
        heat = forcing[0] * closed + (forcing[1] - 0.2 * skin) - f0 - f1
        salt = 0.4 * f1 - forcing[2] * (1.0 - snow)
        melt = 0.5 * heat - 0.8 * (forcing[2] * snow)
        for f, v in enumerate((f2, f3, heat, salt, melt)):
            flux_v[f] = v

        def part(shift, turn):
            slot = (1 + shift) * COLS + lax.rem(col + turn, COLS)
            index = [source_in[slot, pl.ds(8 * h, 8), :] for h in range(2)]
            weight = [weight_in[slot, pl.ds(8 * h, 8), :] for h in range(2)]
            lane = [v & 127 for v in index]
            line = [(v >> 7) - ((1 - shift) * 32 + 8 * col) for v in index]
            sums = [zero] * 10
            for j in range(8):
                here = [line[h] == j for h in range(2)]
                for f in range(5):
                    row = flux_v[f, pl.ds(j, 1), :]
                    for h in range(2):
                        sums[2 * f + h] = jnp.where(here[h], lanes(row, lane[h]), sums[2 * f + h])
            sums = [weight[0] * sums[2 * f] + weight[1] * sums[2 * f + 1] for f in range(5)]
            sums = [v + pltpu.roll(v, 4, 0) for v in sums]
            part_out[step, slot, pl.ds(0, 8), :] = jnp.where(first, sums[0], sums[1])
            part_out[step, slot, pl.ds(8, 8), :] = jnp.where(first, sums[2], sums[3])
            part_out[step, slot, pl.ds(16, 4), :] = sums[4][0:4]
            return part_out.at[step, slot]

        def made(n, shift, turn):
            if step == 0:
                landed(shift, turn, source_in, src_recv)
                landed(shift, turn, weight_in, wt_recv)
            return part(shift, turn)

        send(None, part_in.at[step], part_send.at[step], part_recv.at[step], made)
        part(0, 0)
        push = (f0, f1, -f2, -f3)

        if last:
            def air_result(tile, carry):
                for s in range(8):
                    row = pl.multiple_of(tile * 64 + s * 8, 8)
                    e = ae[pl.ds(row, 8), :]
                    for f in range(4):
                        air_w[pl.ds(f * 512 + tile * 64 + s, 8, stride=8), :] = ay[f, pl.ds(row, 8), :] + e * push[f]
                return carry

            lax.fori_loop(0, LEV // 8, air_result, 0)
            air_copy = pltpu.make_async_copy(air_w, air_o, out_sem.at[0])
            air_copy.start()

        if not last:
            bottom = [ay[f, pl.ds(0, 8), :] + ae[pl.ds(0, 8), :] * push[f] for f in range(4)]
            first_push = push

            def after_first(tile, s):
                row = pl.multiple_of(tile * 64 + s * 8, 8)
                return [ay[f, pl.ds(row, 8), :] + ae[pl.ds(row, 8), :] * first_push[f] for f in range(4)]

            top = air_solve(after_first)

        if last:
            for copy in waiting[:-len(others)]:
                copy.wait_send()
        total = [part_out[step, COLS + col, pl.ds(8 * n, 8 - n // 2 * 4), :] for n in range(3)]
        for shift, turn in others[::-1]:
            slot = landed(shift, turn, part_in.at[step], part_recv.at[step])
            total = [v + part_in[step, slot, pl.ds(8 * n, 8 - n // 2 * 4), :] for n, v in enumerate(total)]

        winds = total[0] * total[0]
        stress = 2.0 * jnp.sqrt(winds + pltpu.roll(winds, 4, 0) + 0.01)
        open_water = 1.0 - ice
        added = open_water * (jnp.where(first, 0.5, 0.3) * total[1])
        sea8[pl.ds(0, 8), :] = sea8[pl.ds(0, 8), :] + jnp.where(wet, added, 0.0)

        def sea_up(n, carry):
            tile = OLEV // 8 - 1 - n
            p, q, w = carry
            for s in range(7, -1, -1):
                row = pl.ds(pl.multiple_of(tile * 64 + s * 8, 8), 8)
                k = smix8[row, :] + stress * sdecay8[row, :]
                b = 1.0 / (1.0 + k)
                a = k * b
                flow = a * q
                q = b * p + flow
                p = p + flow
                w = q * sea8[row, :] + a * w
                sa[row, :] = a
                sb[row, :] = b
                sq[row, :] = q
                sw[row, :] = w
            return p, q, w

        p, q, w = lax.fori_loop(0, OLEV // 8, sea_up, (one, zero, zero))
        surface = jnp.where(wet, w / p, sea8[pl.ds(0, 8), :])
        grown = ice / (ice + open_water * jnp.exp(twice(total[2])))
        ice = jnp.where(wet, grown, ice)
        if not last:
            top_out[step + 1] = jnp.where(first, surface, ice)
            send(top_out.at[step + 1], top_in.at[step + 1], top_send.at[step + 1], top_recv.at[step + 1])
            lax.fori_loop(0, LEV // 8, functools.partial(air_down_again, ag, ab, aw, ay), tuple(top))
        else:
            ice_w[...] = ice[0:4]
            ice_copy = pltpu.make_async_copy(ice_w, ice_o, out_sem.at[2])
            ice_copy.start()

        def sea_level(row, x, q, a, b):
            here = sq[row, :]
            r = 1.0 / q
            x = (a * here * r) * x + (b * r) * sw[row, :]
            return x, here, sa[row, :], sb[row, :]

        def sea_keep(row, tile, s, x):
            x = jnp.where(wet, x, sea8[row, :])
            if last:
                sea_w[pl.ds(tile * 32 + s, 4, stride=8), :] = x[0:4]
                sea_w[pl.ds(320 + tile * 32 + s, 4, stride=8), :] = x[4:8]
            else:
                sea8[row, :] = x

        def sea_down(tile, carry):
            x, q, a, b = carry
            for s in range(8):
                row = pl.ds(pl.multiple_of(tile * 64 + s * 8, 8), 8)
                x, q, a, b = sea_level(row, x, q, a, b)
                sea_keep(row, tile, s, x)
            return x, q, a, b

        row = pl.ds(0, 8)
        sea_keep(row, 0, 0, surface)
        state = (w / p, sq[row, :], sa[row, :], sb[row, :])
        for s in range(1, 8):
            row = pl.ds(s * 8, 8)
            state = sea_level(row, *state)
            sea_keep(row, 0, s, state[0])
        middle = OLEV // 16
        state = lax.fori_loop(1, middle, sea_down, state)
        if last:
            sea_copies = []
            for n in range(2):
                rows = pl.ds(320 * n, 32 * middle)
                sea_copies.append(pltpu.make_async_copy(sea_w.at[rows], sea_o.at[rows], out_sem.at[3 + n]))
                sea_copies[n].start()
        lax.fori_loop(middle, OLEV // 8, sea_down, state)
        if last:
            for n in range(2):
                rows = pl.ds(320 * n + 32 * middle, 320 - 32 * middle)
                sea_copies.append(pltpu.make_async_copy(sea_w.at[rows], sea_o.at[rows], out_sem.at[5 + n]))
                sea_copies[2 + n].start()

    for copy in waiting[-len(others):]:
        copy.wait_send()
    air_copy.wait()
    ice_copy.wait()
    for copy in sea_copies:
        copy.wait()


def air_down_again(ag, ab, aw, ay, tile, carry):
    x = list(carry)
    for s in range(8):
        row = pl.ds(pl.multiple_of(tile * 64 + s * 8, 8), 8)
        g, b = ag[row, :], ab[row, :]
        for f in range(4):
            x[f] = g * x[f] + b * aw[f, row, :]
            ay[f, row, :] = x[f]
    return tuple(x)


def hand_on(air, sea, ice, air_o, sea_o, ice_o, air_v, sea_v, ice_v, sem, out_sem):
    pieces = [(sea, sea_v, sea_o), (ice, ice_v, ice_o)]
    for n in range(4):
        rows = pl.ds(512 * n, 512)
        pieces.append((air.at[rows], air_v.at[rows], air_o.at[rows]))
    into = [pltpu.make_async_copy(src, mid, sem.at[n]) for n, (src, mid, dst) in enumerate(pieces)]
    out = [pltpu.make_async_copy(mid, dst, out_sem.at[n]) for n, (src, mid, dst) in enumerate(pieces)]
    for copy in into:
        copy.start()
    for arrive, leave in zip(into, out):
        arrive.wait()
        leave.start()
    for copy in out:
        copy.wait()


def lines(value):
    levels, columns = value.shape[-2:]
    tall = min(8, levels)
    return value.reshape(-1, tall, columns // 128, 128).swapaxes(1, 2).reshape(-1, 128)


def unlines(rows, shape):
    levels, columns = shape[-2:]
    return rows.reshape(-1, columns // 128, 8, 128).swapaxes(1, 2).reshape(shape)


def per_device(sections, *args):
    air_state, air_mix, forcing, air_mask, osrc, owt, sea_state, sea_mix, ice, sea_mask, asrc, awt = args
    operands = [
        lines(air_state), lines(air_mix), lines(forcing), air_mask.reshape(8, 128), lines(osrc), lines(owt),
        lines(sea_state), lines(sea_mix), ice.reshape(4, 128), sea_mask.reshape(4, 128), lines(asrc), lines(awt),
    ]
    vmem = [pltpu.VMEM(v.shape, v.dtype) for v in operands]
    dma = pltpu.SemaphoreType.DMA
    tall = pltpu.VMEM((8 * OLEV, 128), F32)
    air_one = pltpu.VMEM((8 * LEV, 128), F32)
    air_plus = pltpu.VMEM((8 * LEV + 8, 128), F32)
    air_four = pltpu.VMEM((4, 8 * LEV, 128), F32)
    outs = pl.pallas_call(
        functools.partial(kernel, sections),
        out_shape=[
            jax.ShapeDtypeStruct((2048, 128), F32),
            jax.ShapeDtypeStruct((640, 128), F32),
            jax.ShapeDtypeStruct((4, 128), F32),
        ],
        in_specs=[pl.BlockSpec(memory_space=pltpu.HBM)] * 12,
        out_specs=[pl.BlockSpec(memory_space=pl.ANY)] * 3,
        scratch_shapes=[
            *vmem,
            pltpu.VMEM((STEPS, 8, 128), F32),
            pltpu.VMEM((STEPS, 3 * COLS, 8, 128), F32),
            pltpu.VMEM((5, 8, 128), F32),
            pltpu.VMEM((STEPS, 3 * COLS, 20, 128), F32),
            pltpu.VMEM((STEPS, 3 * COLS, 20, 128), F32),
            pltpu.VMEM((3 * COLS, 16, 128), jnp.int32),
            pltpu.VMEM((3 * COLS, 16, 128), F32),
            tall, tall, tall, tall, tall, tall, tall,
            air_one, air_one, air_plus, air_plus, air_one, air_four, air_four,
            pltpu.VMEM((2048, 128), F32), pltpu.VMEM((640, 128), F32), pltpu.VMEM((4, 128), F32),
            dma((12,)), dma((STEPS, 11)), dma((STEPS, 12)), dma((STEPS, 11)), dma((STEPS, 12)),
            dma((11,)), dma((12,)), dma((11,)), dma((12,)), dma((7,)),
        ],
        compiler_params=pltpu.CompilerParams(collective_id=0, has_side_effects=True, vmem_limit_bytes=60 * 2**20),
        cost_estimate=pl.CostEstimate(flops=20_000_000, bytes_accessed=4_000_000, transcendentals=100_000),
        name="coupled",
    )(*operands)
    outs = pl.pallas_call(
        hand_on,
        out_shape=[jax.ShapeDtypeStruct(v.shape, F32) for v in outs],
        in_specs=[pl.BlockSpec(memory_space=pltpu.HBM)] * 3,
        out_specs=[pl.BlockSpec(memory_space=pltpu.HBM)] * 3,
        scratch_shapes=[*[pltpu.VMEM(v.shape, F32) for v in outs], dma((6,)), dma((6,))],
        compiler_params=pltpu.CompilerParams(vmem_limit_bytes=60 * 2**20),
        cost_estimate=pl.CostEstimate(flops=0, bytes_accessed=3_000_000, transcendentals=0),
        name="hand_on",
    )(*outs)
    return unlines(outs[0], air_state.shape), unlines(outs[1], sea_state.shape), outs[2].reshape(512)


def solution(mesh):
    whole = ("sec", "col")
    deep, flat, line = P(None, None, whole), P(None, whole), P(whole)
    return jax.shard_map(
        functools.partial(per_device, mesh.shape["sec"]),
        mesh=mesh,
        in_specs=(deep, flat, flat, line, flat, flat, deep, flat, line, line, flat, flat),
        out_specs=(deep, deep, line),
        check_vma=False,
    )
```

```python
import functools

import jax
import jax.numpy as jnp
from jax import lax
from jax.experimental import pallas as pl
from jax.experimental.pallas import tpu as pltpu
from jax.sharding import PartitionSpec as P

STEPS = 2
COLS = 4
LEV = 64
OLEV = 80
MESH = pl.DeviceIdType.MESH
F32 = jnp.float32
GATHER = lax.GatherDimensionNumbers(
    offset_dims=(),
    collapsed_slice_dims=(1,),
    start_index_map=(1,),
    operand_batching_dims=(0,),
    start_indices_batching_dims=(0,),
)


def lanes(row, index):
    return lax.gather(
        jnp.broadcast_to(row, (8, 128)),
        index[:, :, None],
        GATHER,
        slice_sizes=(1, 1),
        mode=lax.GatherScatterMode.PROMISE_IN_BOUNDS,
    )


def twice(half):
    return jnp.concatenate([half, half], axis=0)


def kernel(
    sections,
    air_h, amix_h, forcing_h, amask_h, osrc_h, owt_h, sea_h, smix_h, ice_h, smask_h, asrc_h, awt_h,
    air_o, sea_o, ice_o,
    air_v, amix_v, forcing_v, amask_v, osrc_v, owt_v, sea_v, smix_v, ice_v, smask_v, asrc_v, awt_v,
    top_out, top_in, flux_v, part_out, part_in, cells_in,
    smix8, sdecay8, sea8, sq, sw, sa, sb,
    aq, aa, ag, ab, ae, ay, aw, air_w, sea_w, ice_w,
    load_sem, top_send, top_recv, part_send, part_recv, src_send, src_recv, out_sem,
):
    sec = lax.axis_index("sec")
    col = lax.axis_index("col")

    def peer(shift, turn):
        return (lax.rem(sec + shift + sections, sections), lax.rem(col + turn, COLS))

    others = [(-1, 2), (1, 2), (-1, 1), (1, 1), (-1, 3), (1, 3), (0, 2), (-1, 0), (1, 0), (0, 1), (0, 3)]

    barrier = pltpu.get_barrier_semaphore()
    for place in others:
        pl.semaphore_signal(barrier, inc=1, device_id=peer(*place), device_id_type=MESH)

    loads = [
        pltpu.make_async_copy(src, dst, load_sem.at[i])
        for i, (src, dst) in enumerate(
            [
                (sea_h, sea_v), (ice_h, ice_v), (osrc_h, osrc_v), (owt_h, owt_v),
                (forcing_h, forcing_v), (amask_h, amask_v), (amix_h, amix_v), (air_h, air_v),
                (smix_h, smix_v), (smask_h, smask_v),
                (asrc_h, asrc_v), (awt_h, awt_v),
            ]
        )
    ]
    for load in loads:
        load.start()

    one = jnp.ones((8, 128), F32)
    zero = jnp.zeros((8, 128), F32)
    first = lax.broadcasted_iota(jnp.int32, (8, 128), 0) < 4
    waiting = []

    def send(block, places, send_sem, recv_sem, make=None):
        for n, (shift, turn) in enumerate(others):
            slot = (1 - shift) * COLS + col
            copy = pltpu.make_async_remote_copy(
                src_ref=make(n, shift, turn) if make else block,
                dst_ref=places.at[slot],
                send_sem=send_sem.at[n],
                recv_sem=recv_sem.at[slot],
                device_id=peer(shift, turn),
                device_id_type=MESH,
            )
            copy.start()
            waiting.append(copy)

    def landed(shift, turn, places, recv_sem):
        slot = (1 + shift) * COLS + lax.rem(col + turn, COLS)
        block = places.at[slot]
        pltpu.make_async_copy(block, block, recv_sem.at[slot]).wait()
        return slot

    def arrivals(step, places, recv_sem, read, count):
        def one_turn(turn, sums):
            for shift in (0, -1, 1):
                slot = (1 + shift) * COLS + lax.rem(col + turn, COLS)
                if shift or not isinstance(turn, int):
                    landed(shift, turn, places.at[step], recv_sem.at[step])
                sums = read(slot, sums)
            return sums

        sums = one_turn(0, (zero,) * count)
        return lax.fori_loop(1, COLS, lambda n, sums: one_turn(n + n // 2 - 2 * (n // 3), sums), sums)

    loads[0].wait()
    loads[1].wait()
    top_out[0] = jnp.concatenate([sea_v[pl.ds(0, 4, stride=8), :], ice_v[...]], axis=0)
    pl.semaphore_wait(barrier, len(others))
    send(top_out.at[0], top_in.at[0], top_send.at[0], top_recv.at[0])
    loads[10].wait()
    loads[11].wait()
    for n, rows in enumerate((asrc_v, awt_v)):
        four = [rows[pl.ds(k, 4, stride=4), :].astype(F32) for k in range(4)]
        cells_in[COLS + col, n] = jnp.concatenate(four, axis=0)
    send(cells_in.at[COLS + col], cells_in, src_send, src_recv)

    for load in loads[2:10]:
        load.wait()

    def air_up(n, carry):
        tile = 7 - n
        p, q = carry
        for s in range(7, -1, -1):
            k = amix_v[pl.ds(tile * 64 + s, 8, stride=8), :]
            b = 1.0 / (1.0 + k)
            a = k * b
            aq_next = q
            flow = a * q
            q = b * p + flow
            p = p + flow
            level = pl.ds(pl.multiple_of(tile * 64 + s * 8, 8), 8)
            below = pl.ds(pl.multiple_of(tile * 64 + s * 8 + 8, 8), 8)
            aq[level, :] = q
            aa[level, :] = a
            r = 1.0 / q
            ag[below, :] = a * aq_next * r
            ab[below, :] = b * r
        return p, q

    pa, qa = lax.fori_loop(0, LEV // 8, air_up, (one, zero))
    inv_pa = 1.0 / pa

    def air_solve(load):
        def up(n, w):
            tile = 7 - n
            w = list(w)
            for s in range(7, -1, -1):
                row = pl.multiple_of(tile * 64 + s * 8, 8)
                q, a = aq[pl.ds(row, 8), :], aa[pl.ds(row, 8), :]
                e = load(tile, s)
                for f in range(4):
                    w[f] = q * e[f] + a * w[f]
                    aw[f, pl.ds(row, 8), :] = w[f]
            return tuple(w)

        return [v * inv_pa for v in lax.fori_loop(0, LEV // 8, up, (zero,) * 4)]

    def from_start(tile, s):
        return [air_v[pl.ds(f * 512 + tile * 64 + s, 8, stride=8), :] for f in range(4)]

    top = air_solve(from_start)
    unit = qa * inv_pa

    def air_down(tile, carry):
        x, e = list(carry[:4]), carry[4]
        for s in range(8):
            row = pl.multiple_of(tile * 64 + s * 8, 8)
            g, b = ag[pl.ds(row, 8), :], ab[pl.ds(row, 8), :]
            for f in range(4):
                x[f] = g * x[f] + b * aw[f, pl.ds(row, 8), :]
                ay[f, pl.ds(row, 8), :] = x[f]
            e = g * e
            ae[pl.ds(row, 8), :] = e
        return (*x, e)

    ag[pl.ds(0, 8), :] = one
    ab[pl.ds(0, 8), :] = zero
    lax.fori_loop(0, LEV // 8, air_down, (*top, unit))

    def sea_prepare(tile, carry):
        decay = jnp.exp(jnp.full((8, 128), -tile.astype(F32)))
        for s in range(8):
            row = pl.ds(pl.multiple_of(tile * 64 + s * 8, 8), 8)
            k = twice(smix_v[pl.ds(tile * 32 + s, 4, stride=8), :])
            smix8[row, :] = k
            sdecay8[row, :] = k * (decay * jnp.exp(jnp.full((8, 128), -s / 8.0, F32)))
            sea8[row, :] = jnp.concatenate(
                [sea_v[pl.ds(tile * 32 + s, 4, stride=8), :], sea_v[pl.ds(320 + tile * 32 + s, 4, stride=8), :]], axis=0
            )
        return carry

    lax.fori_loop(0, OLEV // 8, sea_prepare, 0)
    wet = twice(smask_v[...]) == 1
    ice = twice(ice_v[...])

    over_sea = amask_v[...] == 1
    forcing = [forcing_v[pl.ds(f, 8, stride=4), :] for f in range(4)]
    bottom = [air_v[pl.ds(f * 512, 8, stride=8), :] for f in range(4)]

    push = None
    for step in range(STEPS):
        last = step == STEPS - 1
        top_in[step, COLS + col] = top_out[step]
        source = [osrc_v[pl.ds(k, 8, stride=4), :] for k in range(4)]
        lane = [v & 127 for v in source]
        line = [v >> 7 for v in source]
        def read_top(slot, sums):
            sums = list(sums)
            for c in range(4):
                t, i = top_in[step, slot, pl.ds(c, 1), :], top_in[step, slot, pl.ds(4 + c, 1), :]
                for k in range(4):
                    here = line[k] == slot * 4 + c
                    sums[k] = jnp.where(here, lanes(t, lane[k]), sums[k])
                    sums[4 + k] = jnp.where(here, lanes(i, lane[k]), sums[4 + k])
            return tuple(sums)

        picked = arrivals(step, top_in, top_recv, read_top, 8)
        temps, ices = picked[:4], picked[4:]
        weight = [owt_v[pl.ds(k, 8, stride=4), :] for k in range(4)]
        warm = (weight[0] * temps[0] + weight[1] * temps[1]) + (weight[2] * temps[2] + weight[3] * temps[3])
        cold = (weight[0] * ices[0] + weight[1] * ices[1]) + (weight[2] * ices[2] + weight[3] * ices[3])

        skin = jnp.where(over_sea, warm, forcing[3])
        frozen = jnp.where(over_sea, cold, 0.0)
        closed = 1.0 / (1.0 + frozen)
        speed = jnp.sqrt(bottom[2] * bottom[2] + bottom[3] * bottom[3] + 1.0)
        coef = 0.3 * speed * closed
        snow = 1.0 / (1.0 + jnp.exp(2.0 * skin))
        f0 = coef * (skin - bottom[0])
        f1 = coef * (0.5 * jnp.exp(0.3 * skin) - bottom[1])
        f2 = coef * bottom[2]
        f3 = coef * bottom[3]
        heat = forcing[0] * closed + (forcing[1] - 0.2 * skin) - f0 - f1
        salt = 0.4 * f1 - forcing[2] * (1.0 - snow)
        melt = 0.5 * heat - 0.8 * (forcing[2] * snow)
        for f, v in enumerate((f2, f3, heat, salt, melt)):
            flux_v[f] = v

        def part(shift, turn):
            slot = (1 + shift) * COLS + lax.rem(col + turn, COLS)
            index = [cells_in[slot, 0, pl.ds(8 * h, 8), :].astype(jnp.int32) for h in range(2)]
            weight = [cells_in[slot, 1, pl.ds(8 * h, 8), :] for h in range(2)]
            lane = [v & 127 for v in index]
            line = [(v >> 7) - ((1 - shift) * 32 + 8 * col) for v in index]
            sums = [zero] * 10
            for j in range(8):
                here = [line[h] == j for h in range(2)]
                for f in range(5):
                    row = flux_v[f, pl.ds(j, 1), :]
                    for h in range(2):
                        sums[2 * f + h] = jnp.where(here[h], lanes(row, lane[h]), sums[2 * f + h])
            sums = [weight[0] * sums[2 * f] + weight[1] * sums[2 * f + 1] for f in range(5)]
            sums = [v + pltpu.roll(v, 4, 0) for v in sums]
            part_out[step, slot, pl.ds(0, 8), :] = jnp.where(first, sums[0], sums[1])
            part_out[step, slot, pl.ds(8, 8), :] = jnp.where(first, sums[2], sums[3])
            part_out[step, slot, pl.ds(16, 4), :] = sums[4][0:4]
            return part_out.at[step, slot]

        def made(n, shift, turn):
            if step == 0:
                landed(shift, turn, cells_in, src_recv)
            return part(shift, turn)

        send(None, part_in.at[step], part_send.at[step], part_recv.at[step], made)
        part(0, 0)
        push = (f0, f1, -f2, -f3)

        if last:
            def air_result(tile, carry):
                for s in range(8):
                    row = pl.multiple_of(tile * 64 + s * 8, 8)
                    e = ae[pl.ds(row, 8), :]
                    for f in range(4):
                        air_w[pl.ds(f * 512 + tile * 64 + s, 8, stride=8), :] = ay[f, pl.ds(row, 8), :] + e * push[f]
                return carry

            lax.fori_loop(0, LEV // 8, air_result, 0)
            air_copy = pltpu.make_async_copy(air_w, air_o, out_sem.at[0])
            air_copy.start()

        if not last:
            bottom = [ay[f, pl.ds(0, 8), :] + ae[pl.ds(0, 8), :] * push[f] for f in range(4)]
            first_push = push

            def after_first(tile, s):
                row = pl.multiple_of(tile * 64 + s * 8, 8)
                return [ay[f, pl.ds(row, 8), :] + ae[pl.ds(row, 8), :] * first_push[f] for f in range(4)]

            top = air_solve(after_first)

        if last:
            for copy in waiting[:-len(others)]:
                copy.wait_send()
        total = [part_out[step, COLS + col, pl.ds(8 * n, 8 - n // 2 * 4), :] for n in range(3)]
        for shift, turn in others[::-1]:
            slot = landed(shift, turn, part_in.at[step], part_recv.at[step])
            total = [v + part_in[step, slot, pl.ds(8 * n, 8 - n // 2 * 4), :] for n, v in enumerate(total)]

        winds = total[0] * total[0]
        stress = 2.0 * jnp.sqrt(winds + pltpu.roll(winds, 4, 0) + 0.01)
        open_water = 1.0 - ice
        added = open_water * (jnp.where(first, 0.5, 0.3) * total[1])
        sea8[pl.ds(0, 8), :] = sea8[pl.ds(0, 8), :] + jnp.where(wet, added, 0.0)

        def sea_up(n, carry):
            tile = OLEV // 8 - 1 - n
            p, q, w = carry
            for s in range(7, -1, -1):
                row = pl.ds(pl.multiple_of(tile * 64 + s * 8, 8), 8)
                k = smix8[row, :] + stress * sdecay8[row, :]
                b = 1.0 / (1.0 + k)
                a = k * b
                flow = a * q
                q = b * p + flow
                p = p + flow
                w = q * sea8[row, :] + a * w
                sa[row, :] = a
                sb[row, :] = b
                sq[row, :] = q
                sw[row, :] = w
            return p, q, w

        p, q, w = lax.fori_loop(0, OLEV // 8, sea_up, (one, zero, zero))
        surface = jnp.where(wet, w / p, sea8[pl.ds(0, 8), :])
        grown = ice / (ice + open_water * jnp.exp(twice(total[2])))
        ice = jnp.where(wet, grown, ice)
        if not last:
            top_out[step + 1] = jnp.where(first, surface, ice)
            send(top_out.at[step + 1], top_in.at[step + 1], top_send.at[step + 1], top_recv.at[step + 1])
            lax.fori_loop(0, LEV // 8, functools.partial(air_down_again, ag, ab, aw, ay), tuple(top))
        else:
            ice_w[...] = ice[0:4]
            ice_copy = pltpu.make_async_copy(ice_w, ice_o, out_sem.at[2])
            ice_copy.start()

        def sea_level(row, x, q, a, b):
            here = sq[row, :]
            r = 1.0 / q
            x = (a * here * r) * x + (b * r) * sw[row, :]
            return x, here, sa[row, :], sb[row, :]

        def sea_keep(row, tile, s, x):
            x = jnp.where(wet, x, sea8[row, :])
            if last:
                sea_w[pl.ds(tile * 32 + s, 4, stride=8), :] = x[0:4]
                sea_w[pl.ds(320 + tile * 32 + s, 4, stride=8), :] = x[4:8]
            else:
                sea8[row, :] = x

        def sea_down(tile, carry):
            x, q, a, b = carry
            for s in range(8):
                row = pl.ds(pl.multiple_of(tile * 64 + s * 8, 8), 8)
                x, q, a, b = sea_level(row, x, q, a, b)
                sea_keep(row, tile, s, x)
            return x, q, a, b

        row = pl.ds(0, 8)
        sea_keep(row, 0, 0, surface)
        state = (w / p, sq[row, :], sa[row, :], sb[row, :])
        for s in range(1, 8):
            row = pl.ds(s * 8, 8)
            state = sea_level(row, *state)
            sea_keep(row, 0, s, state[0])
        middle = OLEV // 16
        state = lax.fori_loop(1, middle, sea_down, state)
        if last:
            sea_copies = []
            for n in range(2):
                rows = pl.ds(320 * n, 32 * middle)
                sea_copies.append(pltpu.make_async_copy(sea_w.at[rows], sea_o.at[rows], out_sem.at[3 + n]))
                sea_copies[n].start()
        lax.fori_loop(middle, OLEV // 8, sea_down, state)
        if last:
            for n in range(2):
                rows = pl.ds(320 * n + 32 * middle, 320 - 32 * middle)
                sea_copies.append(pltpu.make_async_copy(sea_w.at[rows], sea_o.at[rows], out_sem.at[5 + n]))
                sea_copies[2 + n].start()

    for copy in waiting[-len(others):]:
        copy.wait_send()
    air_copy.wait()
    ice_copy.wait()
    for copy in sea_copies:
        copy.wait()


def air_down_again(ag, ab, aw, ay, tile, carry):
    x = list(carry)
    for s in range(8):
        row = pl.ds(pl.multiple_of(tile * 64 + s * 8, 8), 8)
        g, b = ag[row, :], ab[row, :]
        for f in range(4):
            x[f] = g * x[f] + b * aw[f, row, :]
            ay[f, row, :] = x[f]
    return tuple(x)


def hand_on(air, sea, ice, air_o, sea_o, ice_o, air_v, sea_v, ice_v, sem, out_sem):
    pieces = [(sea, sea_v, sea_o), (ice, ice_v, ice_o)]
    for n in range(8):
        rows = pl.ds(256 * n, 256)
        pieces.append((air.at[rows], air_v.at[rows], air_o.at[rows]))
    into = [pltpu.make_async_copy(src, mid, sem.at[n]) for n, (src, mid, dst) in enumerate(pieces)]
    out = [pltpu.make_async_copy(mid, dst, out_sem.at[n]) for n, (src, mid, dst) in enumerate(pieces)]
    for copy in into:
        copy.start()
    for arrive, leave in zip(into, out):
        arrive.wait()
        leave.start()
    for copy in out:
        copy.wait()


def lines(value):
    levels, columns = value.shape[-2:]
    tall = min(8, levels)
    return value.reshape(-1, tall, columns // 128, 128).swapaxes(1, 2).reshape(-1, 128)


def unlines(rows, shape):
    levels, columns = shape[-2:]
    return rows.reshape(-1, columns // 128, 8, 128).swapaxes(1, 2).reshape(shape)


def per_device(sections, *args):
    air_state, air_mix, forcing, air_mask, osrc, owt, sea_state, sea_mix, ice, sea_mask, asrc, awt = args
    operands = [
        lines(air_state), lines(air_mix), lines(forcing), air_mask.reshape(8, 128), lines(osrc), lines(owt),
        lines(sea_state), lines(sea_mix), ice.reshape(4, 128), sea_mask.reshape(4, 128), lines(asrc), lines(awt),
    ]
    vmem = [pltpu.VMEM(v.shape, v.dtype) for v in operands]
    dma = pltpu.SemaphoreType.DMA
    tall = pltpu.VMEM((8 * OLEV, 128), F32)
    air_one = pltpu.VMEM((8 * LEV, 128), F32)
    air_plus = pltpu.VMEM((8 * LEV + 8, 128), F32)
    air_four = pltpu.VMEM((4, 8 * LEV, 128), F32)
    outs = pl.pallas_call(
        functools.partial(kernel, sections),
        out_shape=[
            jax.ShapeDtypeStruct((2048, 128), F32),
            jax.ShapeDtypeStruct((640, 128), F32),
            jax.ShapeDtypeStruct((4, 128), F32),
        ],
        in_specs=[pl.BlockSpec(memory_space=pltpu.HBM)] * 12,
        out_specs=[pl.BlockSpec(memory_space=pl.ANY)] * 3,
        scratch_shapes=[
            *vmem,
            pltpu.VMEM((STEPS, 8, 128), F32),
            pltpu.VMEM((STEPS, 3 * COLS, 8, 128), F32),
            pltpu.VMEM((5, 8, 128), F32),
            pltpu.VMEM((STEPS, 3 * COLS, 20, 128), F32),
            pltpu.VMEM((STEPS, 3 * COLS, 20, 128), F32),
            pltpu.VMEM((3 * COLS, 2, 16, 128), F32),
            tall, tall, tall, tall, tall, tall, tall,
            air_one, air_one, air_plus, air_plus, air_one, air_four, air_four,
            pltpu.VMEM((2048, 128), F32), pltpu.VMEM((640, 128), F32), pltpu.VMEM((4, 128), F32),
            dma((12,)), dma((STEPS, 11)), dma((STEPS, 12)), dma((STEPS, 11)), dma((STEPS, 12)),
            dma((11,)), dma((12,)), dma((7,)),
        ],
        compiler_params=pltpu.CompilerParams(collective_id=0, has_side_effects=True, vmem_limit_bytes=60 * 2**20),
        cost_estimate=pl.CostEstimate(flops=20_000_000, bytes_accessed=4_000_000, transcendentals=100_000),
        name="coupled",
    )(*operands)
    outs = pl.pallas_call(
        hand_on,
        out_shape=[jax.ShapeDtypeStruct(v.shape, F32) for v in outs],
        in_specs=[pl.BlockSpec(memory_space=pltpu.HBM)] * 3,
        out_specs=[pl.BlockSpec(memory_space=pltpu.HBM)] * 3,
        scratch_shapes=[*[pltpu.VMEM(v.shape, F32) for v in outs], dma((10,)), dma((10,))],
        compiler_params=pltpu.CompilerParams(vmem_limit_bytes=60 * 2**20),
        cost_estimate=pl.CostEstimate(flops=0, bytes_accessed=3_000_000, transcendentals=0),
        name="hand_on",
    )(*outs)
    return unlines(outs[0], air_state.shape), unlines(outs[1], sea_state.shape), outs[2].reshape(512)


def solution(mesh):
    whole = ("sec", "col")
    deep, flat, line = P(None, None, whole), P(None, whole), P(whole)
    return jax.shard_map(
        functools.partial(per_device, mesh.shape["sec"]),
        mesh=mesh,
        in_specs=(deep, flat, flat, line, flat, flat, deep, flat, line, line, flat, flat),
        out_specs=(deep, deep, line),
        check_vma=False,
    )
```
